32 devices in a mesh: seq: 2 (over y), exp: 16 (over z, x, core).
Axes of the slice: x: 2, y: 2, z: 4, core: 2. Of those that a mesh axis runs over, the one named last changes fastest.
Arguments:
- stream_input: bfloat16 [16, 256, 2048], P('exp', 'seq'), may hold values from -40 to 40
- grad_output: bfloat16 [16, 256, 2048], P('exp', 'seq'), may hold values from -6 to 6
- norm_gain: float32 [2048], replicated, may hold values from 0.1 to 1.9
- routes: int32 [16, 256, 6], P('exp', 'seq'), may hold values from 0 to 15, all different within a row; in each aligned block of 128 rows (0 to 127, 128 to 255, ..., all dimensions but the last counted through in order) at most 57 rows name the same one
- gates: float32 [16, 256, 6], P('exp', 'seq'), may hold values from 0.1 to 0.6
- w_gate: bfloat16 [16, 2048, 704], P('exp'), may hold values from -0.125 to 0.125
- w_up: bfloat16 [16, 2048, 704], P('exp'), may hold values from -0.125 to 0.125
- w_down: bfloat16 [16, 704, 2048], P('exp'), may hold values from -0.21875 to 0.21875
- ssd_input: bfloat16 [16, 256, 2048], P('exp', 'seq'), may hold values from -0.75 to 0.75
- in_keys: bfloat16 [16, 256, 128], P('exp', 'seq'), may hold values from -6 to 6
- out_queries: bfloat16 [16, 256, 128], P('exp', 'seq'), may hold values from -0.03125 to 0.03125
- log_decay: float32 [16, 256, 32], P('exp', 'seq'), may hold values from -1 to 0
Outputs:
- grad_stream: bfloat16 [16, 256, 2048], P('exp', 'seq')
- grad_x: bfloat16 [16, 256, 2048], P('exp', 'seq')
- grad_b: float32 [16, 256, 128], P('exp', 'seq')
The draws below stay inside these ranges and needn't reach their ends.
Inputs may be any that keep to these rules, and one draw needn't show every extreme that they name: `routes`: each token names 6 different experts; among the 128 tokens of one device no expert is named more than 57 times, a bound that some block reaches.
All inputs are finite; a program needn't handle non-finite values.
Results may differ from the reference program's by a relative error of at most 0.0075.
Values may be sent and summed in bfloat16 or wider, within the bound.
A program may use at most 128 MiB of HBM per device.

```python
import math
import jax
import jax.numpy as jnp
import numpy as np
from jax import lax

D = 2048
SPACE_HEADS = 32
P_SIZE = 64
N = 128
F = 704
TOPK = 6
T_DEV = 128
SEQUENCE_LENGTH = 256
SEQUENCE_COUNT = 16
EXPERTS = 16
CAP = 57


def draw_stream_input(key, part):
    base_key = jax.random.fold_in(key, 11)
    row_key = jax.random.fold_in(key, 12)
    column_key = jax.random.fold_in(key, 13)
    place_key = jax.random.fold_in(key, 15)
    value_entries = jax.random.normal(base_key, (SEQUENCE_COUNT, SEQUENCE_LENGTH, D), jnp.float32)
    row_scale = jnp.exp(jax.random.uniform(row_key, (SEQUENCE_COUNT, SEQUENCE_LENGTH, 1), jnp.float32, -1.15, 1.15))
    value_entries = jnp.clip(value_entries, -6.0, 6.0)
    column_scale = jnp.exp(jax.random.uniform(column_key, (1, 1, D), jnp.float32, -1.15, 1.15)) / 1.47
    value_entries = jnp.clip(value_entries * row_scale * column_scale, -40.0, 40.0)
    seq_pick = jax.random.randint(jax.random.fold_in(place_key, 1), (), 0, SEQUENCE_COUNT)
    row_pick = jax.random.randint(jax.random.fold_in(place_key, 2), (), 0, SEQUENCE_LENGTH)
    column_pick = jax.random.randint(jax.random.fold_in(place_key, 3), (), 0, D)
    value_entries = value_entries.at[seq_pick, row_pick, column_pick].set(40.0)
    value_entries = value_entries.at[seq_pick, row_pick, (column_pick + 1) % D].set(-40.0)
    return value_entries.astype(jnp.bfloat16)


def draw_log_decay(key, part):
    choose_key = jax.random.fold_in(key, 21)
    fast_key = jax.random.fold_in(key, 22)
    slow_key = jax.random.fold_in(key, 23)
    block_key = jax.random.fold_in(key, 24)
    rough_key = jax.random.fold_in(key, 25)
    spike_key = jax.random.fold_in(key, 26)
    depth_random_key = jax.random.fold_in(key, 27)
    block_count = SEQUENCE_LENGTH // T_DEV
    fast_heads = jax.random.uniform(choose_key, (SEQUENCE_COUNT, 1, SPACE_HEADS), jnp.float32) < 0.5
    fast_rate = -jnp.exp(jax.random.uniform(fast_key, (SEQUENCE_COUNT, 1, SPACE_HEADS), jnp.float32, jnp.log(0.04), jnp.log(0.08)))
    slow_rate = -jax.random.uniform(slow_key, (SEQUENCE_COUNT, 1, SPACE_HEADS), jnp.float32, 0.1, 0.6) / SEQUENCE_LENGTH
    rates = jnp.where(fast_heads, fast_rate, slow_rate)
    block_factor = jnp.exp(jax.random.uniform(block_key, (SEQUENCE_COUNT, block_count, 1, SPACE_HEADS), jnp.float32, -0.7, 0.7))
    rough_factor = jnp.exp(jax.random.uniform(rough_key, (SEQUENCE_COUNT, SEQUENCE_LENGTH, SPACE_HEADS), jnp.float32, -0.5, 0.5))
    value_entries = ((rates * rough_factor).reshape(SEQUENCE_COUNT, block_count, T_DEV, SPACE_HEADS) * block_factor).reshape(SEQUENCE_COUNT, SEQUENCE_LENGTH, SPACE_HEADS)
    spike_list = jax.random.uniform(spike_key, (SEQUENCE_COUNT, SEQUENCE_LENGTH, SPACE_HEADS), jnp.float32) < 2.0 / SEQUENCE_LENGTH
    spike_depth = jnp.log(jax.random.uniform(depth_random_key, (SEQUENCE_COUNT, SEQUENCE_LENGTH, SPACE_HEADS), jnp.float32, 0.5, 0.8))
    return value_entries + jnp.where(spike_list, spike_depth, 0.0)


def block_levels(key, dims, shards, smallest, high):
    loudness, own = 1.0, jax.random.fold_in(key, 6)
    for axis_at, shards_of in shards:
        steps = jnp.exp(jax.random.uniform(jax.random.fold_in(own, axis_at), (shards_of,), jnp.float32, smallest / len(shards), high / len(shards)))
        loudness = loudness * jnp.repeat(steps, dims[axis_at] // shards_of).reshape([-1 if axis == axis_at else 1 for axis in range(len(dims))])
    return loudness


def deal_out(own_key, own, number, rows, amount, top, bound, lean):
    ranking = jax.random.permutation(own_key, amount)
    crowded, usual = portions_of(amount, rows * top, bound, lean, True), portions_of(amount, rows * top, bound, lean, False)
    places = jnp.arange(amount)

    def named(sizes, rotation):
        used = int((sizes > 0).sum())
        fixed = max(1, used // 4)
        passed = fixed + (places - fixed + rotation * (used - fixed)) % max(1, amount - fixed)
        return jnp.zeros((amount,), jnp.int32).at[ranking[jnp.where(places < fixed, places, passed)]].set(jnp.asarray(sizes, jnp.int32))

    sizes = jnp.where(number % 4 == 0, named(crowded, number // 4), named(usual, number - number // 4 - 1))
    mixed = jax.random.permutation(jax.random.fold_in(own, 3), amount)
    donor, taker = mixed[0:amount // 2 * 2:2], mixed[1:amount // 2 * 2:2]
    room = jnp.minimum(sizes[donor] - 1, bound - sizes[taker]) // 2
    room = jnp.where((donor == ranking[0]) | (taker == ranking[0]) | (sizes[taker] == 0), 0, jnp.maximum(room, 0))
    passed = jax.random.randint(jax.random.fold_in(own, 4), (amount // 2,), 0, 1 << 20) % (room + 1)
    sizes = sizes.at[donor].add(-passed).at[taker].add(passed)
    items = jnp.searchsorted(jnp.cumsum(sizes), jnp.arange(rows * top), side="right").astype(jnp.int32)
    listing = items.reshape(top, rows).T
    listing = listing[jax.random.permutation(jax.random.fold_in(own, 1), rows)]
    rotation = jax.random.randint(jax.random.fold_in(own, 2), (rows, 1), 0, top)
    return jnp.take_along_axis(listing, (jnp.arange(top)[None, :] + rotation) % top, axis=1)


def portions_of(number_of, total, reach, slope, full):
    loads = [(1 << 20) // math.isqrt(grade ** slope) + 1 for grade in range(1, number_of + 1)]
    largest = reach if full else min(reach, max(-(-total // number_of), total * loads[0] // sum(loads)))
    least = 1 if total - largest >= number_of - 1 else 0
    counts, surplus = [largest] + [least] * (number_of - 1), total - largest - least * (number_of - 1)
    while surplus > 0:
        free = [i for i in range(1, number_of) if counts[i] < largest] or [i for i in range(1, number_of) if counts[i] < reach]
        mass, left = sum([loads[i] for i in free]), surplus
        for i in free:
            addition = min(reach - counts[i], max(1, left * loads[i] // mass), surplus)
            counts[i] = counts[i] + addition
            surplus = surplus - addition
    return np.array(counts)


def centred(stream_key, dims, width, most, pieces=(), kind=jnp.bfloat16):
    entries = jax.random.normal(stream_key, dims, jnp.float32) * width
    if len(pieces) > 0:
        entries = block_levels(stream_key, dims, pieces, -0.22, 0.18) * entries
    return jnp.clip(entries, min=-most, max=most).astype(kind)


def setup_inputs(seed: int = 0) -> dict:
    arg_keys = jax.random.split(jax.random.key(seed), 13)
    stream_input = draw_stream_input(jax.random.fold_in(arg_keys[12], 71), 0)
    grad_output = centred(arg_keys[1], (SEQUENCE_COUNT, SEQUENCE_LENGTH, D), 1.0, 6.0, ((0, 16), (1, 2)))
    norm_gain = jnp.clip(1.0 + 0.18 * jax.random.normal(arg_keys[2], (D,), jnp.float32), 0.1, 1.9)
    routes_keys = jax.random.split(jax.random.fold_in(arg_keys[3], 1), SEQUENCE_COUNT * SEQUENCE_LENGTH // T_DEV)
    routes_turns = jax.random.permutation(jax.random.fold_in(arg_keys[3], 3), SEQUENCE_COUNT * SEQUENCE_LENGTH // T_DEV)
    routes = jax.vmap(lambda own, number: deal_out(jax.random.fold_in(arg_keys[3], 2), own, number, T_DEV, EXPERTS, TOPK, CAP, 1))(routes_keys, routes_turns).reshape((SEQUENCE_COUNT, SEQUENCE_LENGTH, TOPK))
    gates = jnp.clip(0.1 + 0.5 * jax.random.uniform(arg_keys[4], (SEQUENCE_COUNT, SEQUENCE_LENGTH, TOPK), jnp.float32) ** block_levels(arg_keys[4], (SEQUENCE_COUNT, SEQUENCE_LENGTH, TOPK), ((0, 16), (1, 2)), -0.2, 0.2), 0.1, 0.6)
    w_gate = centred(arg_keys[5], (EXPERTS, D, F), D ** -0.5, 0.125, ((0, 16),))
    w_up = centred(arg_keys[6], (EXPERTS, D, F), D ** -0.5, 0.125, ((0, 16),))
    w_down = centred(arg_keys[7], (EXPERTS, F, D), F ** -0.5, 0.21875, ((0, 16),))
    ssd_input = centred(arg_keys[8], (SEQUENCE_COUNT, SEQUENCE_LENGTH, D), P_SIZE ** -0.5, 0.75, ((0, 16), (1, 2)))
    in_keys = centred(arg_keys[9], (SEQUENCE_COUNT, SEQUENCE_LENGTH, N), 1.0, 6.0, ((0, 16), (1, 2)))
    out_queries = centred(arg_keys[10], (SEQUENCE_COUNT, SEQUENCE_LENGTH, N), (SEQUENCE_LENGTH * N) ** -0.5, 0.03125, ((0, 16), (1, 2)))
    log_decay = draw_log_decay(jax.random.fold_in(arg_keys[12], 71), 0)
    return dict(stream_input=stream_input, grad_output=grad_output, norm_gain=norm_gain, routes=routes, gates=gates, w_gate=w_gate, w_up=w_up, w_down=w_down, ssd_input=ssd_input, in_keys=in_keys, out_queries=out_queries, log_decay=log_decay)


EXACT_PRODUCT = lax.Precision.HIGHEST
EPSILON = 1e-05

def assign_slots(flat_routes, expert_count):
    onehot_table = (flat_routes[:, None] == jnp.arange(expert_count, dtype=jnp.int32)[None, :]).astype(jnp.int32)
    earlier_hits = jnp.cumsum(onehot_table, axis=0) - onehot_table
    return lax.optimization_barrier(jnp.sum(earlier_hits * onehot_table, axis=1)).astype(jnp.int32)

def transposed_product(left_rows, weight_matrix):
    return lax.dot_general(left_rows, weight_matrix, (((1,), (1,)), ((), ())), preferred_element_type=jnp.float32)

def expert_back(normed_rows, grad_rows, gate_weight, up_weight, down_weight):
    gate_pre = jnp.dot(normed_rows, gate_weight, preferred_element_type=jnp.float32)
    up_pre = jnp.dot(normed_rows, up_weight, preferred_element_type=jnp.float32)
    back_rows = transposed_product(grad_rows, down_weight)
    sigmoid_gate = jax.nn.sigmoid(gate_pre)
    grad_gate = (back_rows * up_pre * sigmoid_gate * (1.0 + gate_pre * (1.0 - sigmoid_gate))).astype(jnp.bfloat16)
    grad_up = (back_rows * gate_pre * sigmoid_gate).astype(jnp.bfloat16)
    summed = transposed_product(grad_gate, gate_weight) + transposed_product(grad_up, up_weight)
    return summed.astype(jnp.bfloat16)

def block_terms(out_grad, inputs, key_rows, query_rows, decay_rows):
    row_count = out_grad.shape[0]
    head_count = decay_rows.shape[1]
    cum_decay = jnp.cumsum(decay_rows, axis=0)
    by_head = cum_decay.T
    later_mask = (jnp.arange(row_count)[None, :] >= jnp.arange(row_count)[:, None])[None]
    differences = by_head[:, None, :] - by_head[:, :, None]
    decay_matrix = jnp.where(later_mask, jnp.exp(jnp.where(later_mask, differences, -1e+30)), 0.0)
    scores = jnp.dot(key_rows, query_rows.T, precision=EXACT_PRODUCT)
    grad_heads = out_grad.reshape(row_count, head_count, -1)
    input_heads = inputs.reshape(row_count, head_count, -1)
    head_size = grad_heads.shape[2]
    intra_x = jnp.einsum('hts,shp->thp', decay_matrix * scores[None], grad_heads, precision=EXACT_PRODUCT).reshape(row_count, -1)
    pair_mix = jnp.einsum('thp,shp->hts', input_heads, grad_heads, precision=EXACT_PRODUCT)
    intra_b = jnp.dot(lax.optimization_barrier(jnp.sum(decay_matrix * pair_mix, axis=0)), query_rows, precision=EXACT_PRODUCT)
    weighted = out_grad * jnp.repeat(jnp.exp(cum_decay), head_size, axis=1)
    local_state = jnp.dot(query_rows.T, weighted, precision=EXACT_PRODUCT)
    decay_total = cum_decay[-1]
    edge_decay = jnp.repeat(jnp.exp(cum_decay[-1][None, :] - cum_decay), head_size, axis=1)
    return (intra_x, intra_b, local_state, decay_total, edge_decay)

def remote_terms(incoming, key_rows, inputs, edge_decay):
    remote_x = edge_decay * jnp.dot(key_rows, incoming, precision=EXACT_PRODUCT)
    remote_b = jnp.dot(inputs * edge_decay, incoming.T, precision=EXACT_PRODUCT)
    return (remote_x, remote_b)

def pass_back(carried, block_item):
    decay_total, local_state = block_item
    factor = jnp.repeat(jnp.exp(decay_total), local_state.shape[1] // decay_total.shape[0])[None, :]
    return (local_state + factor * carried, carried)

def reference(stream_input, grad_output, norm_gain, routes, gates, w_gate, w_up, w_down, ssd_input, in_keys, out_queries, log_decay):
    token_count = SEQUENCE_COUNT * SEQUENCE_LENGTH
    block_count = token_count // T_DEV
    stream_rows = stream_input.reshape(token_count, D).astype(jnp.float32)
    root_mean = jnp.sqrt(lax.optimization_barrier(jnp.mean(stream_rows * stream_rows, axis=1, keepdims=True)) + EPSILON)
    unit_rows = stream_rows / root_mean
    normed = (unit_rows * norm_gain[None, :]).astype(jnp.bfloat16)
    grad_rows = grad_output.reshape(token_count, D)
    flat_routes = routes.reshape(block_count, T_DEV * TOPK).astype(jnp.int32)
    slots = jax.vmap(lambda block_routes: assign_slots(block_routes, EXPERTS))(flat_routes)
    block_ids = jnp.arange(block_count, dtype=jnp.int32)[:, None]
    positions = ((flat_routes * block_count + block_ids) * CAP + slots).reshape(-1)
    owner_rows = (block_ids * T_DEV + jnp.arange(T_DEV * TOPK, dtype=jnp.int32)[None, :] // TOPK).reshape(-1)
    slot_table = jnp.full((EXPERTS * block_count * CAP,), token_count, jnp.int32).at[positions].set(owner_rows)
    gate_table = jnp.zeros((EXPERTS * block_count * CAP,), jnp.float32).at[positions].set(gates.reshape(-1))
    slot_table = slot_table.reshape(EXPERTS, block_count * CAP)
    gate_table = gate_table.reshape(EXPERTS, block_count * CAP)
    normed_padded = jnp.concatenate([normed, jnp.zeros((1, D), jnp.bfloat16)], axis=0)
    grads_padded = jnp.concatenate([grad_rows, jnp.zeros((1, D), jnp.bfloat16)], axis=0)

    def one_expert(accumulated, expert_item):
        slot_index, slot_gates, gate_weight, up_weight, down_weight = expert_item
        result_rows = expert_back(normed_padded[slot_index], grads_padded[slot_index], gate_weight, up_weight, down_weight)
        return (accumulated.at[slot_index].add(slot_gates[:, None] * result_rows.astype(jnp.float32)), None)
    accumulated, ignored = lax.scan(one_expert, jnp.zeros((token_count + 1, D), jnp.float32), (slot_table, gate_table, w_gate, w_up, w_down))
    normed_grad = accumulated[:token_count]
    scaled = normed_grad * norm_gain[None, :]
    stream_grad = (grad_rows.astype(jnp.float32) + (scaled - unit_rows * lax.optimization_barrier(jnp.mean(unit_rows * scaled, axis=1, keepdims=True))) / root_mean).astype(jnp.bfloat16)
    per_sequence = SEQUENCE_LENGTH // T_DEV
    grads_blocks = stream_grad.reshape(SEQUENCE_COUNT, per_sequence, T_DEV, D).astype(jnp.float32)
    input_blocks = ssd_input.reshape(SEQUENCE_COUNT, per_sequence, T_DEV, D).astype(jnp.float32)
    key_blocks = in_keys.reshape(SEQUENCE_COUNT, per_sequence, T_DEV, N).astype(jnp.float32)
    query_blocks = out_queries.reshape(SEQUENCE_COUNT, per_sequence, T_DEV, N).astype(jnp.float32)
    decay_blocks = log_decay.reshape(SEQUENCE_COUNT, per_sequence, T_DEV, SPACE_HEADS)

    def one_sequence(sequence_item):
        out_grad, inputs, key_rows, query_rows, decay_rows = sequence_item
        intra_x, intra_b, local_state, decay_total, edge_decay = jax.vmap(block_terms)(out_grad, inputs, key_rows, query_rows, decay_rows)
        final_state, incoming = lax.scan(pass_back, jnp.zeros((N, D), jnp.float32), (decay_total, local_state), reverse=True)
        remote_x, remote_b = jax.vmap(remote_terms)(incoming, key_rows, inputs, edge_decay)
        return ((intra_x + remote_x).astype(jnp.bfloat16), intra_b + remote_b)
    grad_x, grad_b = lax.map(one_sequence, (grads_blocks, input_blocks, key_blocks, query_blocks, decay_blocks))
    return (stream_grad.reshape(SEQUENCE_COUNT, SEQUENCE_LENGTH, D), grad_x.reshape(SEQUENCE_COUNT, SEQUENCE_LENGTH, D), grad_b.reshape(SEQUENCE_COUNT, SEQUENCE_LENGTH, N))
```

```python
import functools

import jax
import jax.numpy as jnp
from jax import lax
from jax.experimental import pallas as pl
from jax.experimental.pallas import tpu as pltpu
from jax.sharding import PartitionSpec as P

TOPK = 6
EPSILON = 1e-05
BF16 = jnp.bfloat16
F32 = jnp.float32


def dot(a, b, ca, cb):
    return lax.dot_general(a, b, (((ca,), (cb,)), ((), ())), preferred_element_type=F32)


def intra_kernel(head_count, dy_ref, x_ref, key_ref, query_ref, cum_ref, cumt_ref, gx_ref, gb_ref):
    rows = dy_ref.shape[0]
    size = dy_ref.shape[1] // head_count
    pair = 128 // size
    scores = dot(key_ref[...], query_ref[...], 1, 1)
    t = lax.broadcasted_iota(jnp.int32, (rows, rows), 0)
    s = lax.broadcasted_iota(jnp.int32, (rows, rows), 1)
    later = s >= t
    lane = lax.broadcasted_iota(jnp.int32, (rows, 128), 1) // size
    mixed = jnp.zeros((rows, rows), F32)
    for p in range(head_count // pair):
        columns = slice(p * 128, (p + 1) * 128)
        dy = dy_ref[:, columns]
        x = x_ref[:, columns]
        out = jnp.zeros((rows, 128), F32)
        for q in range(pair):
            h = p * pair + q
            gap = cumt_ref[h : h + 1, :] - cum_ref[:, h : h + 1]
            decay = jnp.where(later, jnp.exp(jnp.where(later, gap, 0.0)), 0.0)
            own = lane == q
            out = jnp.where(own, dot((decay * scores).astype(BF16), dy, 1, 0), out)
            mixed = mixed + decay * dot(jnp.where(own, x, jnp.zeros_like(x)), dy, 1, 1)
        gx_ref[:, columns] = out
    gb_ref[...] = dot(mixed.astype(BF16), query_ref[...], 1, 0)


def intra_terms(dy, inputs, keys, queries, cum):
    rows, width = dy.shape
    return pl.pallas_call(
        functools.partial(intra_kernel, cum.shape[1]),
        out_shape=(
            jax.ShapeDtypeStruct((rows, width), F32),
            jax.ShapeDtypeStruct((rows, keys.shape[1]), F32),
        ),
        cost_estimate=pl.CostEstimate(flops=400_000_000, bytes_accessed=2_500_000, transcendentals=524_288),
        compiler_params=pltpu.CompilerParams(vmem_limit_bytes=24 * 1024 * 1024),
    )(dy, inputs, keys, queries, cum, cum.T)


def incoming_state(total, state):
    count = lax.axis_size("seq")
    if count == 2:
        return lax.ppermute(state.astype(BF16), "seq", [(1, 0)])
    place = lax.axis_index("seq")
    states = lax.all_gather(state.astype(BF16), "seq")
    totals = lax.all_gather(total, "seq")
    carried = jnp.zeros(state.shape, F32)
    repeat = state.shape[1] // total.shape[0]
    for block in range(count - 1, 0, -1):
        factor = jnp.repeat(jnp.exp(totals[block]), repeat)[None, :]
        joined = states[block].astype(F32) + factor * carried
        carried = jnp.where(block > place, joined, carried)
    return carried.astype(BF16)


def local(
    stream_input,
    grad_output,
    norm_gain,
    routes,
    gates,
    w_gate,
    w_up,
    w_down,
    ssd_input,
    in_keys,
    out_queries,
    log_decay,
):
    tokens = stream_input.shape[1]
    width = stream_input.shape[2]
    heads = log_decay.shape[2]
    size = width // heads
    experts = lax.axis_size("exp")
    capacity = -(-(tokens * 7 // experts + 1) // 16) * 16
    stream = stream_input[0].astype(F32)
    root = jnp.sqrt(jnp.mean(stream * stream, axis=1, keepdims=True) + EPSILON)
    unit = stream / root
    normed = (unit * norm_gain[None, :]).astype(BF16)
    grads = grad_output[0]

    names = jnp.arange(experts, dtype=jnp.int32)
    table = jnp.sum(
        jnp.where(routes[0][None] == names[:, None, None], gates[0][None], 0.0), axis=2
    )
    own_gates = lax.all_to_all(table, "exp", split_axis=0, concat_axis=0, tiled=True)
    all_normed = lax.all_gather(normed, "exp")
    all_grads = lax.all_gather(grads, "exp")

    chosen = own_gates > 0.0
    before = jnp.triu(jnp.ones((tokens, tokens), BF16), 1)
    slots = dot(chosen.astype(BF16), before, 1, 0).astype(jnp.int32)
    places = jnp.arange(capacity, dtype=jnp.int32)[None, :, None]
    picks = (slots[:, None, :] == places) & chosen[:, None, :]
    onehot = picks.astype(BF16)
    slot_gates = jnp.sum(jnp.where(picks, own_gates[:, None, :], 0.0), axis=2).reshape(-1, 1)

    def take(rows):
        taken = lax.dot_general(
            onehot, rows, (((2,), (1,)), ((0,), (0,))), preferred_element_type=F32
        )
        return taken.astype(BF16).reshape(experts * capacity, width)

    gate_weight, up_weight, down_weight = w_gate[0], w_up[0], w_down[0]
    normed_rows = take(all_normed)
    gate_pre = dot(normed_rows, gate_weight, 1, 0)
    up_pre = dot(normed_rows, up_weight, 1, 0)
    back = dot(take(all_grads), down_weight, 1, 1)
    sig = jax.nn.sigmoid(gate_pre)
    grad_gate = (back * up_pre * sig * (1.0 + gate_pre * (1.0 - sig))).astype(BF16)
    grad_up = (back * gate_pre * sig).astype(BF16)
    summed = dot(grad_gate, gate_weight, 1, 1) + dot(grad_up, up_weight, 1, 1)
    weighted = (slot_gates * summed).astype(BF16).reshape(experts, capacity, width)
    spread = lax.dot_general(
        onehot, weighted, (((1,), (1,)), ((0,), (0,))), preferred_element_type=F32
    ).astype(BF16)
    normed_grad = lax.psum_scatter(spread, "exp", scatter_dimension=0, tiled=False).astype(F32)

    scaled = normed_grad * norm_gain[None, :]
    dy = (
        grads.astype(F32)
        + (scaled - unit * jnp.mean(unit * scaled, axis=1, keepdims=True)) / root
    ).astype(BF16)

    inputs = ssd_input[0]
    keys, queries = in_keys[0], out_queries[0]
    cum = jnp.dot(
        jnp.tril(jnp.ones((tokens, tokens), F32)), log_decay[0], precision=lax.Precision.HIGHEST
    )
    total = cum[-1]
    growth = jnp.repeat(jnp.exp(cum), size, axis=1)
    edge = jnp.repeat(jnp.exp(total[None, :] - cum), size, axis=1)
    state = dot(queries, (dy.astype(F32) * growth).astype(BF16), 0, 0)
    incoming = incoming_state(total, state)
    intra_x, intra_b = intra_terms(dy, inputs, keys, queries, cum)
    grad_x = (intra_x + edge * dot(keys, incoming, 1, 0)).astype(BF16)
    grad_b = intra_b + dot((inputs.astype(F32) * edge).astype(BF16), incoming, 1, 1)
    return (dy[None], grad_x[None], grad_b[None])


def solution(mesh):
    tokens = P("exp", "seq", None)
    weights = P("exp", None, None)
    return jax.shard_map(
        local,
        mesh=mesh,
        in_specs=(tokens, tokens, P(), tokens, tokens, weights, weights, weights)
        + (tokens,) * 4,
        out_specs=(tokens,) * 3,
        check_vma=False,
    )
```

```python
import functools

import jax
import jax.numpy as jnp
from jax import lax
from jax.experimental import pallas as pl
from jax.experimental.pallas import tpu as pltpu
from jax.sharding import PartitionSpec as P

TOPK = 6
EPSILON = 1e-05
BF16 = jnp.bfloat16
F32 = jnp.float32


def dot(a, b, ca, cb):
    return lax.dot_general(a, b, (((ca,), (cb,)), ((), ())), preferred_element_type=F32)


def intra_kernel(head_count, dy_ref, x_ref, key_ref, query_ref, cum_ref, cumt_ref, gx_ref, gb_ref):
    rows = dy_ref.shape[0]
    size = dy_ref.shape[1] // head_count
    pair = 128 // size
    scores = dot(key_ref[...], query_ref[...], 1, 1)
    t = lax.broadcasted_iota(jnp.int32, (rows, rows), 0)
    s = lax.broadcasted_iota(jnp.int32, (rows, rows), 1)
    later = s >= t
    lane = lax.broadcasted_iota(jnp.int32, (rows, 128), 1) // size
    mixed = jnp.zeros((rows, rows), F32)
    for p in range(head_count // pair):
        columns = slice(p * 128, (p + 1) * 128)
        dy = dy_ref[:, columns]
        x = x_ref[:, columns]
        out = jnp.zeros((rows, 128), F32)
        for q in range(pair):
            h = p * pair + q
            gap = cumt_ref[h : h + 1, :] - cum_ref[:, h : h + 1]
            decay = jnp.where(later, jnp.exp(jnp.where(later, gap, 0.0)), 0.0)
            own = lane == q
            out = jnp.where(own, dot((decay * scores).astype(BF16), dy, 1, 0), out)
            mixed = mixed + decay * dot(jnp.where(own, x, jnp.zeros_like(x)), dy, 1, 1)
        gx_ref[:, columns] = out
    gb_ref[...] = dot(mixed.astype(BF16), query_ref[...], 1, 0)


def intra_terms(dy, inputs, keys, queries, cum):
    rows, width = dy.shape
    return pl.pallas_call(
        functools.partial(intra_kernel, cum.shape[1]),
        out_shape=(
            jax.ShapeDtypeStruct((rows, width), F32),
            jax.ShapeDtypeStruct((rows, keys.shape[1]), F32),
        ),
        cost_estimate=pl.CostEstimate(flops=400_000_000, bytes_accessed=2_500_000, transcendentals=524_288),
        compiler_params=pltpu.CompilerParams(vmem_limit_bytes=24 * 1024 * 1024),
    )(dy, inputs, keys, queries, cum, cum.T)


def incoming_state(total, state):
    count = lax.axis_size("seq")
    if count == 2:
        return lax.ppermute(state.astype(BF16), "seq", [(1, 0)])
    place = lax.axis_index("seq")
    states = lax.all_gather(state.astype(BF16), "seq")
    totals = lax.all_gather(total, "seq")
    carried = jnp.zeros(state.shape, F32)
    repeat = state.shape[1] // total.shape[0]
    for block in range(count - 1, 0, -1):
        factor = jnp.repeat(jnp.exp(totals[block]), repeat)[None, :]
        joined = states[block].astype(F32) + factor * carried
        carried = jnp.where(block > place, joined, carried)
    return carried.astype(BF16)


def local(
    stream_input,
    grad_output,
    norm_gain,
    routes,
    gates,
    w_gate,
    w_up,
    w_down,
    ssd_input,
    in_keys,
    out_queries,
    log_decay,
):
    tokens = stream_input.shape[1]
    width = stream_input.shape[2]
    heads = log_decay.shape[2]
    size = width // heads
    experts = lax.axis_size("exp")
    capacity = -(-(tokens * 7 // experts + 1) // 16) * 16
    stream = stream_input[0].astype(F32)
    root = jnp.sqrt(jnp.mean(stream * stream, axis=1, keepdims=True) + EPSILON)
    unit = stream / root
    normed = (unit * norm_gain[None, :]).astype(BF16)
    grads = grad_output[0]

    names = jnp.arange(experts, dtype=jnp.int32)
    table = jnp.sum(
        jnp.where(routes[0][None] == names[:, None, None], gates[0][None], 0.0), axis=2
    )
    own_gates = lax.all_to_all(table, "exp", split_axis=0, concat_axis=0, tiled=True)
    all_normed = lax.all_gather(normed, "exp")
    all_grads = lax.all_gather(grads, "exp")

    chosen = own_gates > 0.0
    before = jnp.triu(jnp.ones((tokens, tokens), BF16), 1)
    slots = dot(chosen.astype(BF16), before, 1, 0).astype(jnp.int32)
    places = jnp.arange(capacity, dtype=jnp.int32)[None, :, None]
    picks = (slots[:, None, :] == places) & chosen[:, None, :]
    onehot = picks.astype(BF16)
    slot_gates = jnp.sum(jnp.where(picks, own_gates[:, None, :], 0.0), axis=2).reshape(-1, 1)

    def take(rows):
        taken = lax.dot_general(
            onehot, rows, (((2,), (1,)), ((0,), (0,))), preferred_element_type=F32
        )
        return taken.astype(BF16).reshape(experts * capacity, width)

    gate_weight, up_weight, down_weight = w_gate[0], w_up[0], w_down[0]
    normed_rows = take(all_normed)
    gate_pre = dot(normed_rows, gate_weight, 1, 0)
    up_pre = dot(normed_rows, up_weight, 1, 0)
    back = dot(take(all_grads), down_weight, 1, 1)
    sig = jax.nn.sigmoid(gate_pre)
    grad_gate = (back * up_pre * sig * (1.0 + gate_pre * (1.0 - sig))).astype(BF16)
    grad_up = (back * gate_pre * sig).astype(BF16)
    half = width // 2
    parts = []
    for first in (0, half):
        rows = slice(first, first + half)
        summed = dot(grad_gate, gate_weight[rows], 1, 1) + dot(grad_up, up_weight[rows], 1, 1)
        weighted = (slot_gates * summed).astype(BF16).reshape(experts, capacity, half)
        spread = lax.dot_general(
            onehot, weighted, (((1,), (1,)), ((0,), (0,))), preferred_element_type=F32
        ).astype(BF16)
        parts.append(lax.psum_scatter(spread, "exp", scatter_dimension=0, tiled=False))
    normed_grad = jnp.concatenate(parts, axis=1).astype(F32)

    scaled = normed_grad * norm_gain[None, :]
    dy = (
        grads.astype(F32)
        + (scaled - unit * jnp.mean(unit * scaled, axis=1, keepdims=True)) / root
    ).astype(BF16)

    inputs = ssd_input[0]
    keys, queries = in_keys[0], out_queries[0]
    cum = jnp.dot(
        jnp.tril(jnp.ones((tokens, tokens), F32)), log_decay[0], precision=lax.Precision.HIGHEST
    )
    total = cum[-1]
    growth = jnp.repeat(jnp.exp(cum), size, axis=1)
    edge = jnp.repeat(jnp.exp(total[None, :] - cum), size, axis=1)
    state = dot(queries, (dy.astype(F32) * growth).astype(BF16), 0, 0)
    incoming = incoming_state(total, state)
    intra_x, intra_b = intra_terms(dy, inputs, keys, queries, cum)
    grad_x = (intra_x + edge * dot(keys, incoming, 1, 0)).astype(BF16)
    grad_b = intra_b + dot((inputs.astype(F32) * edge).astype(BF16), incoming, 1, 1)
    return (dy[None], grad_x[None], grad_b[None])


def solution(mesh):
    tokens = P("exp", "seq", None)
    weights = P("exp", None, None)
    return jax.shard_map(
        local,
        mesh=mesh,
        in_specs=(tokens, tokens, P(), tokens, tokens, weights, weights, weights)
        + (tokens,) * 4,
        out_specs=(tokens,) * 3,
        check_vma=False,
    )
```

```python
import functools

import jax
import jax.numpy as jnp
from jax import lax
from jax.experimental import pallas as pl
from jax.experimental.pallas import tpu as pltpu
from jax.sharding import PartitionSpec as P

TOPK = 6
EPSILON = 1e-05
BF16 = jnp.bfloat16
F32 = jnp.float32


def dot(a, b, ca, cb):
    return lax.dot_general(a, b, (((ca,), (cb,)), ((), ())), preferred_element_type=F32)


def intra_kernel(head_count, dy_ref, x_ref, key_ref, query_ref, cum_ref, cumt_ref, gx_ref, gb_ref):
    rows = dy_ref.shape[0]
    size = dy_ref.shape[1] // head_count
    pair = 128 // size
    scores = dot(key_ref[...], query_ref[...], 1, 1)
    t = lax.broadcasted_iota(jnp.int32, (rows, rows), 0)
    s = lax.broadcasted_iota(jnp.int32, (rows, rows), 1)
    later = s >= t
    lane = lax.broadcasted_iota(jnp.int32, (rows, 128), 1) // size
    mixed = jnp.zeros((rows, rows), F32)
    for p in range(head_count // pair):
        columns = slice(p * 128, (p + 1) * 128)
        dy = dy_ref[:, columns]
        x = x_ref[:, columns]
        out = jnp.zeros((rows, 128), F32)
        for q in range(pair):
            h = p * pair + q
            gap = cumt_ref[h : h + 1, :] - cum_ref[:, h : h + 1]
            decay = jnp.where(later, jnp.exp(jnp.where(later, gap, 0.0)), 0.0)
            own = lane == q
            out = jnp.where(own, dot((decay * scores).astype(BF16), dy, 1, 0), out)
            mixed = mixed + decay * dot(jnp.where(own, x, jnp.zeros_like(x)), dy, 1, 1)
        gx_ref[:, columns] = out
    gb_ref[...] = dot(mixed.astype(BF16), query_ref[...], 1, 0)


def intra_terms(dy, inputs, keys, queries, cum):
    rows, width = dy.shape
    return pl.pallas_call(
        functools.partial(intra_kernel, cum.shape[1]),
        out_shape=(
            jax.ShapeDtypeStruct((rows, width), F32),
            jax.ShapeDtypeStruct((rows, keys.shape[1]), F32),
        ),
        cost_estimate=pl.CostEstimate(flops=400_000_000, bytes_accessed=2_500_000, transcendentals=524_288),
        compiler_params=pltpu.CompilerParams(vmem_limit_bytes=24 * 1024 * 1024),
    )(dy, inputs, keys, queries, cum, cum.T)


def incoming_state(total, state):
    count = lax.axis_size("seq")
    if count == 2:
        return lax.ppermute(state.astype(BF16), "seq", [(1, 0)])
    place = lax.axis_index("seq")
    states = lax.all_gather(state.astype(BF16), "seq")
    totals = lax.all_gather(total, "seq")
    carried = jnp.zeros(state.shape, F32)
    repeat = state.shape[1] // total.shape[0]
    for block in range(count - 1, 0, -1):
        factor = jnp.repeat(jnp.exp(totals[block]), repeat)[None, :]
        joined = states[block].astype(F32) + factor * carried
        carried = jnp.where(block > place, joined, carried)
    return carried.astype(BF16)


def local(
    stream_input,
    grad_output,
    norm_gain,
    routes,
    gates,
    w_gate,
    w_up,
    w_down,
    ssd_input,
    in_keys,
    out_queries,
    log_decay,
):
    tokens = stream_input.shape[1]
    width = stream_input.shape[2]
    heads = log_decay.shape[2]
    size = width // heads
    experts = lax.axis_size("exp")
    capacity = -(-(tokens * 7 // experts + 1) // 16) * 16
    stream = stream_input[0].astype(F32)
    root = jnp.sqrt(jnp.mean(stream * stream, axis=1, keepdims=True) + EPSILON)
    unit = stream / root
    normed = (unit * norm_gain[None, :]).astype(BF16)
    grads = grad_output[0]

    names = jnp.arange(experts, dtype=jnp.int32)
    table = jnp.sum(
        jnp.where(routes[0][None] == names[:, None, None], gates[0][None], 0.0), axis=2
    )
    own_gates = lax.all_to_all(table, "exp", split_axis=0, concat_axis=0, tiled=True)
    all_normed = lax.all_gather(normed, "exp")

    before = jnp.triu(jnp.ones((tokens, tokens), BF16), 1)
    places = jnp.arange(capacity, dtype=jnp.int32)[None, :, None]

    def picks(weights):
        chosen = weights > 0.0
        slots = dot(chosen.astype(BF16), before, 1, 0).astype(jnp.int32)
        return (slots[:, None, :] == places) & chosen[:, None, :]

    sent = picks(table).astype(BF16).reshape(experts * capacity, tokens)
    send_grads = dot(sent, grads, 1, 0).astype(BF16).reshape(experts, capacity, width)
    grad_rows = lax.all_to_all(send_grads, "exp", split_axis=0, concat_axis=0, tiled=True)
    grad_rows = grad_rows.reshape(experts * capacity, width)

    held = picks(own_gates)
    slot_gates = jnp.sum(jnp.where(held, own_gates[:, None, :], 0.0), axis=2).reshape(-1, 1)
    normed_rows = (
        lax.dot_general(
            held.astype(BF16), all_normed, (((2,), (1,)), ((0,), (0,))), preferred_element_type=F32
        )
        .astype(BF16)
        .reshape(experts * capacity, width)
    )
    gate_weight, up_weight, down_weight = w_gate[0], w_up[0], w_down[0]
    back = dot(grad_rows, down_weight, 1, 1)
    gate_pre = dot(normed_rows, gate_weight, 1, 0)
    up_pre = dot(normed_rows, up_weight, 1, 0)
    sig = jax.nn.sigmoid(gate_pre)
    grad_gate = (back * up_pre * sig * (1.0 + gate_pre * (1.0 - sig))).astype(BF16)
    grad_up = (back * gate_pre * sig).astype(BF16)
    summed = dot(grad_gate, gate_weight, 1, 1) + dot(grad_up, up_weight, 1, 1)
    weighted = (slot_gates * summed).astype(BF16).reshape(experts, capacity, width)
    returned = lax.all_to_all(weighted, "exp", split_axis=0, concat_axis=0, tiled=True)
    normed_grad = dot(sent, returned.reshape(experts * capacity, width), 0, 0)

    scaled = normed_grad * norm_gain[None, :]
    dy = (
        grads.astype(F32)
        + (scaled - unit * jnp.mean(unit * scaled, axis=1, keepdims=True)) / root
    ).astype(BF16)

    inputs = ssd_input[0]
    keys, queries = in_keys[0], out_queries[0]
    cum = jnp.dot(
        jnp.tril(jnp.ones((tokens, tokens), F32)), log_decay[0], precision=lax.Precision.HIGHEST
    )
    total = cum[-1]
    growth = jnp.repeat(jnp.exp(cum), size, axis=1)
    edge = jnp.repeat(jnp.exp(total[None, :] - cum), size, axis=1)
    state = dot(queries, (dy.astype(F32) * growth).astype(BF16), 0, 0)
    incoming = incoming_state(total, state)
    intra_x, intra_b = intra_terms(dy, inputs, keys, queries, cum)
    grad_x = (intra_x + edge * dot(keys, incoming, 1, 0)).astype(BF16)
    grad_b = intra_b + dot((inputs.astype(F32) * edge).astype(BF16), incoming, 1, 1)
    return (dy[None], grad_x[None], grad_b[None])


def solution(mesh):
    tokens = P("exp", "seq", None)
    weights = P("exp", None, None)
    return jax.shard_map(
        local,
        mesh=mesh,
        in_specs=(tokens, tokens, P(), tokens, tokens, weights, weights, weights)
        + (tokens,) * 4,
        out_specs=(tokens,) * 3,
        check_vma=False,
    )
```

```python
import functools

import jax
import jax.numpy as jnp
from jax import lax
from jax.experimental import pallas as pl
from jax.experimental.pallas import tpu as pltpu
from jax.sharding import PartitionSpec as P

TOPK = 6
EPSILON = 1e-05
BF16 = jnp.bfloat16
F32 = jnp.float32


def dot(a, b, ca, cb):
    return lax.dot_general(a, b, (((ca,), (cb,)), ((), ())), preferred_element_type=F32)


def intra_kernel(head_count, dy_ref, x_ref, key_ref, query_ref, cum_ref, cumt_ref, gx_ref, gb_ref):
    rows = dy_ref.shape[0]
    size = dy_ref.shape[1] // head_count
    pair = 128 // size
    scores = dot(key_ref[...], query_ref[...], 1, 1)
    t = lax.broadcasted_iota(jnp.int32, (rows, rows), 0)
    s = lax.broadcasted_iota(jnp.int32, (rows, rows), 1)
    later = s >= t
    lane = lax.broadcasted_iota(jnp.int32, (rows, 128), 1) // size
    mixed = jnp.zeros((rows, rows), F32)
    for p in range(head_count // pair):
        columns = slice(p * 128, (p + 1) * 128)
        dy = dy_ref[:, columns]
        x = x_ref[:, columns]
        out = jnp.zeros((rows, 128), F32)
        for q in range(pair):
            h = p * pair + q
            gap = cumt_ref[h : h + 1, :] - cum_ref[:, h : h + 1]
            decay = jnp.where(later, jnp.exp(jnp.where(later, gap, 0.0)), 0.0)
            own = lane == q
            out = jnp.where(own, dot((decay * scores).astype(BF16), dy, 1, 0), out)
            mixed = mixed + decay * dot(jnp.where(own, x, jnp.zeros_like(x)), dy, 1, 1)
        gx_ref[:, columns] = out
    gb_ref[...] = dot(mixed.astype(BF16), query_ref[...], 1, 0)


def intra_terms(dy, inputs, keys, queries, cum):
    rows, width = dy.shape
    return pl.pallas_call(
        functools.partial(intra_kernel, cum.shape[1]),
        out_shape=(
            jax.ShapeDtypeStruct((rows, width), F32),
            jax.ShapeDtypeStruct((rows, keys.shape[1]), F32),
        ),
        cost_estimate=pl.CostEstimate(flops=400_000_000, bytes_accessed=2_500_000, transcendentals=524_288),
        compiler_params=pltpu.CompilerParams(vmem_limit_bytes=24 * 1024 * 1024),
    )(dy, inputs, keys, queries, cum, cum.T)


def incoming_state(total, state):
    count = lax.axis_size("seq")
    if count == 2:
        return lax.ppermute(state.astype(BF16), "seq", [(1, 0)])
    place = lax.axis_index("seq")
    states = lax.all_gather(state.astype(BF16), "seq")
    totals = lax.all_gather(total, "seq")
    carried = jnp.zeros(state.shape, F32)
    repeat = state.shape[1] // total.shape[0]
    for block in range(count - 1, 0, -1):
        factor = jnp.repeat(jnp.exp(totals[block]), repeat)[None, :]
        joined = states[block].astype(F32) + factor * carried
        carried = jnp.where(block > place, joined, carried)
    return carried.astype(BF16)


def gather_beside(rows):
    count = lax.axis_size("exp")
    if count != 16:
        return lax.all_gather(rows, "exp")
    depth = count // 4
    me = lax.axis_index("exp")
    z, x, core = me // 4, (me // 2) % 2, me % 2
    out = jnp.zeros((depth, 2, 2) + rows.shape, rows.dtype)
    for step in range(depth):
        block = rows
        if step:
            block = lax.ppermute(rows, "exp", [(i, (i + 4 * step) % count) for i in range(count)])
        other = lax.ppermute(block, "exp", [(i, i ^ 2) for i in range(count)])
        pair = jnp.where(x == 0, jnp.stack([block, other]), jnp.stack([other, block]))
        swapped = lax.ppermute(pair, "exp", [(i, i ^ 1) for i in range(count)])
        quad = jnp.where(
            core == 0, jnp.stack([pair, swapped], 1), jnp.stack([swapped, pair], 1)
        )
        out = lax.dynamic_update_index_in_dim(out, quad, (z - step + depth) % depth, 0)
    return out.reshape((count,) + rows.shape)


def local(
    stream_input,
    grad_output,
    norm_gain,
    routes,
    gates,
    w_gate,
    w_up,
    w_down,
    ssd_input,
    in_keys,
    out_queries,
    log_decay,
):
    tokens = stream_input.shape[1]
    width = stream_input.shape[2]
    heads = log_decay.shape[2]
    size = width // heads
    experts = lax.axis_size("exp")
    capacity = -(-(tokens * 7 // experts + 1) // 16) * 16
    stream = stream_input[0].astype(F32)
    root = jnp.sqrt(jnp.mean(stream * stream, axis=1, keepdims=True) + EPSILON)
    unit = stream / root
    normed = (unit * norm_gain[None, :]).astype(BF16)
    grads = grad_output[0]

    names = jnp.arange(experts, dtype=jnp.int32)
    table = jnp.sum(
        jnp.where(routes[0][None] == names[:, None, None], gates[0][None], 0.0), axis=2
    )
    own_gates = lax.all_to_all(table, "exp", split_axis=0, concat_axis=0, tiled=True)
    all_normed = lax.all_gather(normed, "exp")

    before = jnp.triu(jnp.ones((tokens, tokens), BF16), 1)
    places = jnp.arange(capacity, dtype=jnp.int32)[None, :, None]

    def picks(weights):
        chosen = weights > 0.0
        slots = dot(chosen.astype(BF16), before, 1, 0).astype(jnp.int32)
        return (slots[:, None, :] == places) & chosen[:, None, :]

    sent = picks(table).astype(BF16).reshape(experts * capacity, tokens)
    all_grads = gather_beside(grads)

    held = picks(own_gates)
    slot_gates = jnp.sum(jnp.where(held, own_gates[:, None, :], 0.0), axis=2).reshape(-1, 1)
    onehot = held.astype(BF16)

    def take(rows):
        taken = lax.dot_general(
            onehot, rows, (((2,), (1,)), ((0,), (0,))), preferred_element_type=F32
        )
        return taken.astype(BF16).reshape(experts * capacity, width)

    normed_rows = take(all_normed)
    grad_rows = take(all_grads)
    gate_weight, up_weight, down_weight = w_gate[0], w_up[0], w_down[0]
    back = dot(grad_rows, down_weight, 1, 1)
    gate_pre = dot(normed_rows, gate_weight, 1, 0)
    up_pre = dot(normed_rows, up_weight, 1, 0)
    sig = jax.nn.sigmoid(gate_pre)
    grad_gate = (back * up_pre * sig * (1.0 + gate_pre * (1.0 - sig))).astype(BF16)
    grad_up = (back * gate_pre * sig).astype(BF16)
    summed = dot(grad_gate, gate_weight, 1, 1) + dot(grad_up, up_weight, 1, 1)
    weighted = (slot_gates * summed).astype(BF16).reshape(experts, capacity, width)
    returned = lax.all_to_all(weighted, "exp", split_axis=0, concat_axis=0, tiled=True)
    normed_grad = dot(sent, returned.reshape(experts * capacity, width), 0, 0)

    scaled = normed_grad * norm_gain[None, :]
    dy = (
        grads.astype(F32)
        + (scaled - unit * jnp.mean(unit * scaled, axis=1, keepdims=True)) / root
    ).astype(BF16)

    inputs = ssd_input[0]
    keys, queries = in_keys[0], out_queries[0]
    cum = jnp.dot(
        jnp.tril(jnp.ones((tokens, tokens), F32)), log_decay[0], precision=lax.Precision.HIGHEST
    )
    total = cum[-1]
    growth = jnp.repeat(jnp.exp(cum), size, axis=1)
    edge = jnp.repeat(jnp.exp(total[None, :] - cum), size, axis=1)
    state = dot(queries, (dy.astype(F32) * growth).astype(BF16), 0, 0)
    incoming = incoming_state(total, state)
    intra_x, intra_b = intra_terms(dy, inputs, keys, queries, cum)
    grad_x = (intra_x + edge * dot(keys, incoming, 1, 0)).astype(BF16)
    grad_b = intra_b + dot((inputs.astype(F32) * edge).astype(BF16), incoming, 1, 1)
    return (dy[None], grad_x[None], grad_b[None])


def solution(mesh):
    tokens = P("exp", "seq", None)
    weights = P("exp", None, None)
    return jax.shard_map(
        local,
        mesh=mesh,
        in_specs=(tokens, tokens, P(), tokens, tokens, weights, weights, weights)
        + (tokens,) * 4,
        out_specs=(tokens,) * 3,
        check_vma=False,
    )
```

```python
import functools

import jax
import jax.numpy as jnp
from jax import lax
from jax.experimental import pallas as pl
from jax.experimental.pallas import tpu as pltpu
from jax.sharding import PartitionSpec as P

TOPK = 6
EPSILON = 1e-05
BF16 = jnp.bfloat16
F32 = jnp.float32


def dot(a, b, ca, cb):
    return lax.dot_general(a, b, (((ca,), (cb,)), ((), ())), preferred_element_type=F32)


def intra_kernel(head_count, dy_ref, x_ref, key_ref, query_ref, cum_ref, cumt_ref, gx_ref, gb_ref):
    rows = dy_ref.shape[0]
    size = dy_ref.shape[1] // head_count
    pair = 128 // size
    scores = dot(key_ref[...], query_ref[...], 1, 1)
    t = lax.broadcasted_iota(jnp.int32, (rows, rows), 0)
    s = lax.broadcasted_iota(jnp.int32, (rows, rows), 1)
    later = s >= t
    lane = lax.broadcasted_iota(jnp.int32, (rows, 128), 1) // size
    mixed = jnp.zeros((rows, rows), F32)
    for p in range(head_count // pair):
        columns = slice(p * 128, (p + 1) * 128)
        dy = dy_ref[:, columns]
        x = x_ref[:, columns]
        out = jnp.zeros((rows, 128), F32)
        for q in range(pair):
            h = p * pair + q
            gap = cumt_ref[h : h + 1, :] - cum_ref[:, h : h + 1]
            decay = jnp.where(later, jnp.exp(jnp.where(later, gap, 0.0)), 0.0)
            own = lane == q
            out = jnp.where(own, dot((decay * scores).astype(BF16), dy, 1, 0), out)
            mixed = mixed + decay * dot(jnp.where(own, x, jnp.zeros_like(x)), dy, 1, 1)
        gx_ref[:, columns] = out
    gb_ref[...] = dot(mixed.astype(BF16), query_ref[...], 1, 0)


def intra_terms(dy, inputs, keys, queries, cum):
    rows, width = dy.shape
    return pl.pallas_call(
        functools.partial(intra_kernel, cum.shape[1]),
        out_shape=(
            jax.ShapeDtypeStruct((rows, width), F32),
            jax.ShapeDtypeStruct((rows, keys.shape[1]), F32),
        ),
        cost_estimate=pl.CostEstimate(flops=400_000_000, bytes_accessed=2_500_000, transcendentals=524_288),
        compiler_params=pltpu.CompilerParams(vmem_limit_bytes=24 * 1024 * 1024),
    )(dy, inputs, keys, queries, cum, cum.T)


def incoming_state(total, state):
    count = lax.axis_size("seq")
    if count == 2:
        return lax.ppermute(state.astype(BF16), "seq", [(1, 0)])
    place = lax.axis_index("seq")
    states = lax.all_gather(state.astype(BF16), "seq")
    totals = lax.all_gather(total, "seq")
    carried = jnp.zeros(state.shape, F32)
    repeat = state.shape[1] // total.shape[0]
    for block in range(count - 1, 0, -1):
        factor = jnp.repeat(jnp.exp(totals[block]), repeat)[None, :]
        joined = states[block].astype(F32) + factor * carried
        carried = jnp.where(block > place, joined, carried)
    return carried.astype(BF16)


def gather_groups(rows):
    count = lax.axis_size("exp")
    if count != 16:
        return [lax.all_gather(rows, "exp")]
    x, core = (lax.axis_index("exp") // 2) % 2, lax.axis_index("exp") % 2
    groups = []
    for step in range(count // 4):
        block = rows
        if step:
            block = lax.ppermute(rows, "exp", [(i, (i + 4 * step) % count) for i in range(count)])
        other = lax.ppermute(block, "exp", [(i, i ^ 2) for i in range(count)])
        pair = jnp.where(x == 0, jnp.stack([block, other]), jnp.stack([other, block]))
        swapped = lax.ppermute(pair, "exp", [(i, i ^ 1) for i in range(count)])
        quad = jnp.where(
            core == 0, jnp.stack([pair, swapped], 1), jnp.stack([swapped, pair], 1)
        )
        groups.append(quad.reshape((4,) + rows.shape))
    return groups


def regroup(array, groups):
    if groups == 1:
        return array
    own = lax.axis_index("exp") // (array.shape[0] // groups)
    parted = array.reshape((groups, array.shape[0] // groups) + array.shape[1:])
    picked = [
        lax.dynamic_index_in_dim(parted, lax.rem(own - g + groups, groups), 0)
        for g in range(groups)
    ]
    return jnp.concatenate(picked).reshape(array.shape)


def local(
    stream_input,
    grad_output,
    norm_gain,
    routes,
    gates,
    w_gate,
    w_up,
    w_down,
    ssd_input,
    in_keys,
    out_queries,
    log_decay,
):
    tokens = stream_input.shape[1]
    width = stream_input.shape[2]
    heads = log_decay.shape[2]
    size = width // heads
    experts = lax.axis_size("exp")
    capacity = -(-(tokens * 7 // experts + 1) // 16) * 16
    stream = stream_input[0].astype(F32)
    root = jnp.sqrt(jnp.mean(stream * stream, axis=1, keepdims=True) + EPSILON)
    unit = stream / root
    normed = (unit * norm_gain[None, :]).astype(BF16)
    grads = grad_output[0]

    names = jnp.arange(experts, dtype=jnp.int32)
    table = jnp.sum(
        jnp.where(routes[0][None] == names[:, None, None], gates[0][None], 0.0), axis=2
    )
    own_gates = lax.all_to_all(table, "exp", split_axis=0, concat_axis=0, tiled=True)
    all_normed = gather_groups(normed)

    before = jnp.triu(jnp.ones((tokens, tokens), BF16), 1)
    places = jnp.arange(capacity, dtype=jnp.int32)[None, :, None]

    def picks(weights):
        chosen = weights > 0.0
        slots = dot(chosen.astype(BF16), before, 1, 0).astype(jnp.int32)
        return (slots[:, None, :] == places) & chosen[:, None, :]

    sent = picks(table).astype(BF16).reshape(experts * capacity, tokens)
    all_grads = gather_groups(grads)
    groups = len(all_grads)
    own_gates = regroup(own_gates, groups)

    held = picks(own_gates)
    slot_gates = jnp.sum(jnp.where(held, own_gates[:, None, :], 0.0), axis=2).reshape(-1, 1)
    onehot = held.astype(BF16)

    each = experts // groups

    def take(blocks):
        taken = [
            lax.dot_general(
                onehot[g * each : (g + 1) * each],
                rows,
                (((2,), (1,)), ((0,), (0,))),
                preferred_element_type=F32,
            ).astype(BF16)
            for g, rows in enumerate(blocks)
        ]
        return jnp.concatenate(taken).reshape(experts * capacity, width)

    normed_rows = take(all_normed)
    grad_rows = take(all_grads)
    gate_weight, up_weight, down_weight = w_gate[0], w_up[0], w_down[0]
    back = dot(grad_rows, down_weight, 1, 1)
    gate_pre = dot(normed_rows, gate_weight, 1, 0)
    up_pre = dot(normed_rows, up_weight, 1, 0)
    sig = jax.nn.sigmoid(gate_pre)
    grad_gate = (back * up_pre * sig * (1.0 + gate_pre * (1.0 - sig))).astype(BF16)
    grad_up = (back * gate_pre * sig).astype(BF16)
    summed = dot(grad_gate, gate_weight, 1, 1) + dot(grad_up, up_weight, 1, 1)
    weighted = (slot_gates * summed).astype(BF16).reshape(experts, capacity, width)
    weighted = regroup(weighted, groups)
    returned = lax.all_to_all(weighted, "exp", split_axis=0, concat_axis=0, tiled=True)
    normed_grad = dot(sent, returned.reshape(experts * capacity, width), 0, 0)

    scaled = normed_grad * norm_gain[None, :]
    dy = (
        grads.astype(F32)
        + (scaled - unit * jnp.mean(unit * scaled, axis=1, keepdims=True)) / root
    ).astype(BF16)

    inputs = ssd_input[0]
    keys, queries = in_keys[0], out_queries[0]
    cum = jnp.dot(
        jnp.tril(jnp.ones((tokens, tokens), F32)), log_decay[0], precision=lax.Precision.HIGHEST
    )
    total = cum[-1]
    growth = jnp.repeat(jnp.exp(cum), size, axis=1)
    edge = jnp.repeat(jnp.exp(total[None, :] - cum), size, axis=1)
    state = dot(queries, (dy.astype(F32) * growth).astype(BF16), 0, 0)
    incoming = incoming_state(total, state)
    intra_x, intra_b = intra_terms(dy, inputs, keys, queries, cum)
    grad_x = (intra_x + edge * dot(keys, incoming, 1, 0)).astype(BF16)
    grad_b = intra_b + dot((inputs.astype(F32) * edge).astype(BF16), incoming, 1, 1)
    return (dy[None], grad_x[None], grad_b[None])


def solution(mesh):
    tokens = P("exp", "seq", None)
    weights = P("exp", None, None)
    return jax.shard_map(
        local,
        mesh=mesh,
        in_specs=(tokens, tokens, P(), tokens, tokens, weights, weights, weights)
        + (tokens,) * 4,
        out_specs=(tokens,) * 3,
        check_vma=False,
    )
```
